32 devices in a mesh: ctx: 8 (over z, x), tp: 4 (over y, core).
Axes of the slice: x: 2, y: 2, z: 4, core: 2. Of those that a mesh axis runs over, the one named last changes fastest.
Arguments:
- queries: bfloat16 [4096, 5120], P(('ctx', 'tp')), may hold values from -400 to 400
- keys: bfloat16 [4096, 5120], P(('ctx', 'tp')), may hold values from -6 to 6
- values: bfloat16 [4096, 5120], P(('ctx', 'tp')), may hold values from -6 to 6
- dout: bfloat16 [4096, 5120], P(('ctx', 'tp')), may hold values from -6 to 6
- match: int32 [10, 16], replicated, may hold values from 0 to 15, as said below
Outputs:
- attended: bfloat16 [4096, 5120], P(('ctx', 'tp'))
- grad_queries: bfloat16 [4096, 5120], P(('ctx', 'tp'))
- grad_keys: bfloat16 [4096, 5120], P(('ctx', 'tp'))
- grad_values: bfloat16 [4096, 5120], P(('ctx', 'tp'))
The draws below stay inside these ranges and needn't reach their ends.
Inputs may be any that keep to these rules, and one draw needn't show every extreme that they name: match[g, i] lies in 0 to i; the value i means that query block i has no matched block for group g. Among the 20 pairs of a query block and a group of one ctx index, at most 1 name a block of the tokens of any one other ctx index, and 1 is reached.
All inputs are finite; a program needn't handle non-finite values.
Results may differ from the reference program's by a relative error of at most 0.025.
Values may be sent and summed in bfloat16 or wider, within the bound.
A program may use at most 128 MiB of HBM per device.

```python
import jax
import jax.numpy as jnp
from jax import lax

HEADS = 40
HEAD_DIM = 128
BLOCK = 256
GROUPS = 10
CAP = 1
SEQ = 4096
NB = 16
NB_DEV = 2
WIDTH = 5120


def draw_match(key, part):
    total_blocks = NB
    per_device = NB_DEV
    ctx_count = NB // NB_DEV
    block_ids = jnp.arange(total_blocks, dtype=jnp.int32)
    target = block_ids // per_device
    position = block_ids % per_device
    first_draw = jax.random.randint(jax.random.fold_in(key, 1), (GROUPS, total_blocks), 0, 1 << 20, dtype=jnp.int32)
    second_draw = jax.random.randint(jax.random.fold_in(key, 2), (GROUPS, total_blocks), 0, 1 << 20, dtype=jnp.int32)
    third_draw = jax.random.randint(jax.random.fold_in(key, 3), (GROUPS, total_blocks), 0, 1 << 20, dtype=jnp.int32)
    span_size = target + 1
    source = first_draw % span_size * (second_draw % span_size) // jnp.maximum(target, 1)
    local_pick = target * per_device + third_draw % jnp.maximum(position, 1)
    local_pick = jnp.where(position > 0, local_pick, block_ids)
    far_pick = source * per_device + third_draw % per_device
    remote = source < target
    source_t = source.T.reshape(ctx_count, per_device * GROUPS)
    remote_t = remote.T.reshape(ctx_count, per_device * GROUPS)
    onehot = ((source_t[:, :, None] == jnp.arange(ctx_count, dtype=jnp.int32)) & remote_t[:, :, None]).astype(jnp.int32)
    before = jnp.cumsum(onehot, axis=1) - onehot
    slot_rank = jnp.sum(before * onehot, axis=2)
    kept_t = remote_t & (slot_rank < CAP)
    kept = kept_t.reshape(total_blocks, GROUPS).T
    chosen = jnp.where(remote, jnp.where(kept, far_pick, block_ids), local_pick)
    group_ids = jnp.arange(GROUPS, dtype=jnp.int32)
    last_mark = (group_ids[:, None] == 0) & (block_ids[None, :] == total_blocks - 1)
    chosen = jnp.where(last_mark, block_ids[None, :], chosen)
    return chosen.astype(jnp.int32)


def base_keys(key):
    noise = jax.random.normal(jax.random.fold_in(key, 7), (SEQ, HEADS * HEAD_DIM), jnp.float32)
    return jnp.clip(noise, -6.0, 6.0)


def draw_keys(key, part):
    basis = base_keys(key)
    return basis.astype(jnp.bfloat16)


def draw_queries(key, part):
    fresh = jnp.clip(jax.random.normal(jax.random.fold_in(key, 8), (SEQ, HEADS * HEAD_DIM), jnp.float32), -6.0, 6.0)
    return fresh.astype(jnp.bfloat16)


def shard_levels(own_key, shape, split, least, largest):
    factor_of = 1.0
    for axis_at, blocks in split:
        steps = jax.random.uniform(jax.random.fold_in(jax.random.fold_in(own_key, 6), axis_at), (blocks,), jnp.float32, least / len(split), largest / len(split))
        factor_of = factor_of * jnp.repeat(jnp.exp(steps), shape[axis_at] // blocks).reshape((-1,) + (1,) * (len(shape) - 1 - axis_at))
    return factor_of


def normal_values(rng, shape, deviation, bound, split=(), held_as=jnp.bfloat16):
    entries = deviation * jax.random.normal(rng, shape, jnp.float32)
    if split:
        entries = entries * shard_levels(rng, shape, split, -0.22, 0.18)
    return jnp.clip(entries, -bound, bound).astype(held_as)


def setup_inputs(seed: int = 0) -> dict:
    seeds = jax.random.split(jax.random.key(seed), 6)
    queries = draw_queries(jax.random.fold_in(seeds[5], 71), 0)
    keys = draw_keys(jax.random.fold_in(seeds[5], 71), 0)
    values = normal_values(seeds[2], (SEQ, WIDTH), 1.0, 6.0, ((0, 32),))
    dout = normal_values(seeds[3], (SEQ, WIDTH), 1.0, 6.0, ((0, 32),))
    match = draw_match(jax.random.fold_in(seeds[5], 71), 0)
    return {"queries": queries, "keys": keys, "values": values, "dout": dout, "match": match}


def reference(queries, keys, values, dout, match):
    score_scale = HEAD_DIM ** -0.5
    total_blocks = queries.shape[0] // BLOCK

    def split_blocks(array):
        return array.reshape(total_blocks, BLOCK, HEADS, HEAD_DIM)

    q_all = split_blocks(queries)
    k_all = split_blocks(keys)
    v_all = split_blocks(values)
    d_all = split_blocks(dout)
    head_ids = jnp.arange(HEADS, dtype=jnp.int32)
    head_match = match[head_ids % GROUPS, :]
    causal = jnp.arange(BLOCK)[:, None] >= jnp.arange(BLOCK)[None, :]

    def to_bf16_f32(array):
        rounded = lax.optimization_barrier(array.astype(jnp.bfloat16))
        return rounded.astype(jnp.float32)

    def step(carry, index):
        acc_k, acc_v = carry
        q_blk = lax.dynamic_index_in_dim(q_all, index, 0, keepdims=False).astype(jnp.float32)
        k_own = lax.dynamic_index_in_dim(k_all, index, 0, keepdims=False).astype(jnp.float32)
        v_own = lax.dynamic_index_in_dim(v_all, index, 0, keepdims=False).astype(jnp.float32)
        d_blk = lax.dynamic_index_in_dim(d_all, index, 0, keepdims=False).astype(jnp.float32)
        partner = lax.dynamic_index_in_dim(head_match, index, 1, keepdims=False)
        is_valid = partner < index
        far_k = k_all[partner, :, head_ids, :].astype(jnp.float32)
        far_v = v_all[partner, :, head_ids, :].astype(jnp.float32)
        s_own = jnp.einsum('qhd,khd->hqk', q_blk, k_own) * score_scale
        s_own = jnp.where(causal[None], s_own, -jnp.inf)
        s_far = jnp.einsum('qhd,hkd->hqk', q_blk, far_k) * score_scale
        s_far = jnp.where(is_valid[:, None, None], s_far, -jnp.inf)
        row_top = jnp.maximum(jnp.max(s_own, axis=-1), jnp.max(s_far, axis=-1))
        row_total = jnp.sum(jnp.exp(s_own - row_top[..., None]), axis=-1) + jnp.sum(jnp.exp(s_far - row_top[..., None]), axis=-1)
        log_total = row_top + jnp.log(row_total)
        p_own = jnp.exp(s_own - log_total[..., None])
        p_far = jnp.exp(s_far - log_total[..., None])
        pb_own = to_bf16_f32(p_own)
        pb_far = to_bf16_f32(p_far)
        attended = jnp.einsum('hqk,khd->qhd', pb_own, v_own) + jnp.einsum('hqk,hkd->qhd', pb_far, far_v)
        out_blk = attended.astype(jnp.bfloat16)
        delta = jnp.sum(d_blk * out_blk.astype(jnp.float32), axis=-1).T
        dp_own = jnp.einsum('qhd,khd->hqk', d_blk, v_own)
        dp_far = jnp.einsum('qhd,hkd->hqk', d_blk, far_v)
        ds_own = to_bf16_f32(p_own * (dp_own - delta[..., None]) * score_scale)
        ds_far = to_bf16_f32(p_far * (dp_far - delta[..., None]) * score_scale)
        grad_q = jnp.einsum('hqk,khd->qhd', ds_own, k_own) + jnp.einsum('hqk,hkd->qhd', ds_far, far_k)
        gk_own = jnp.einsum('hqk,qhd->khd', ds_own, q_blk)
        gv_own = jnp.einsum('hqk,qhd->khd', pb_own, d_blk)
        gk_far = jnp.einsum('hqk,qhd->hkd', ds_far, q_blk)
        gv_far = jnp.einsum('hqk,qhd->hkd', pb_far, d_blk)
        acc_k = acc_k.at[index].add(gk_own)
        acc_v = acc_v.at[index].add(gv_own)
        acc_k = acc_k.at[partner, :, head_ids, :].add(gk_far)
        acc_v = acc_v.at[partner, :, head_ids, :].add(gv_far)
        return (acc_k, acc_v), (out_blk, grad_q.astype(jnp.bfloat16))

    zeros_acc = jnp.zeros((total_blocks, BLOCK, HEADS, HEAD_DIM), jnp.float32)
    (acc_k, acc_v), (outs, grads_q) = lax.scan(step, (zeros_acc, zeros_acc), jnp.arange(total_blocks, dtype=jnp.int32))
    full_shape = (total_blocks * BLOCK, HEADS * HEAD_DIM)
    return (outs.reshape(full_shape), grads_q.reshape(full_shape), acc_k.astype(jnp.bfloat16).reshape(full_shape), acc_v.astype(jnp.bfloat16).reshape(full_shape))
```

```python
import functools

import jax
import jax.numpy as jnp
from jax import lax
from jax.experimental import pallas as pl
from jax.experimental.pallas import tpu as pltpu
from jax.sharding import PartitionSpec as P

HEAD_DIM = 128
BLOCK = 256
GROUPS = 10
MESH = pl.DeviceIdType.MESH
LOG2E = 1.4426950408889634


def dot(a, b, dims):
    return lax.dot_general(a, b, ((dims[:1], dims[1:]), ((), ())), preferred_element_type=jnp.float32)


def kernel(
    n,
    ctxs,
    match,
    q_ref,
    k_ref,
    v_ref,
    d_ref,
    att_ref,
    gq_ref,
    gk_ref,
    gv_ref,
    qb,
    kb,
    vb,
    db,
    attb,
    gqb,
    gkb,
    gvb,
    gk32,
    gv32,
    gfar,
    pack,
    slots,
    back,
    came,
    table,
    in_send,
    kv_recv,
    qd_recv,
    in_local,
    slot_send,
    slot_recv,
    ret_send,
    ret_recv,
    out_send,
    out_recv,
    out_local,
):
    c = lax.axis_index("ctx")
    me = lax.axis_index("tp")
    part = q_ref.shape[0]
    width = qb.shape[1]
    here = qb.shape[0] // BLOCK
    heads = width // HEAD_DIM
    shares = BLOCK // part
    peers = [lax.rem(me + d, n) for d in range(1, n)]

    def rows_of(j):
        return pl.ds(pl.multiple_of(j * part, part), part)

    def cols_of(j):
        return pl.ds(pl.multiple_of(j * width, width), width)

    def head_of(g):
        return pl.ds(pl.multiple_of(g * HEAD_DIM, HEAD_DIM), HEAD_DIM)

    def wide_head(j, g):
        return pl.ds(pl.multiple_of(j * width + g * HEAD_DIM, HEAD_DIM), HEAD_DIM)

    ins = (q_ref, k_ref, v_ref, d_ref)
    bufs = (qb, kb, vb, db)
    outs = (att_ref, gq_ref, gk_ref, gv_ref)
    stages = (attb, gqb, gkb, gvb)

    def own_in(x):
        return pltpu.make_async_copy(
            ins[x].at[:, cols_of(me)], bufs[x].at[rows_of(me), :], in_local.at[x]
        )

    for x in (0, 3):
        own_in(x).start()

    def kv_place(x, j, g):
        half = pl.multiple_of(lax.rem(j, shares) * part, part)
        return bufs[x].at[(j // shares) * heads + g, pl.ds(half, part), :]

    def own_kv(x, g):
        return pltpu.make_async_copy(
            ins[x].at[:, wide_head(me, g)], kv_place(x, me, g), in_local.at[x]
        )

    def start_own_kv(g, carry):
        for x in (1, 2):
            own_kv(x, g).start()
        return carry

    lax.fori_loop(0, heads, start_own_kv, 0)

    barrier = pltpu.get_barrier_semaphore()
    for j in peers:
        pl.semaphore_signal(barrier, inc=1, device_id=(c, j), device_id_type=MESH)

    def greet(step, carry):
        pl.semaphore_signal(
            barrier, inc=1, device_id=(lax.rem(c + step, ctxs), me), device_id_type=MESH
        )
        return carry

    lax.fori_loop(1, ctxs, greet, 0)
    pl.semaphore_wait(barrier, n - 1 + ctxs - 1)

    def kv_copy(x, j, g, row):
        return pltpu.make_async_remote_copy(
            src_ref=ins[x].at[:, wide_head(j, g)],
            dst_ref=kv_place(x, row, g),
            send_sem=in_send.at[x, j],
            recv_sem=kv_recv.at[x - 1, g, row],
            device_id=(c, j),
            device_id_type=MESH,
        )

    def send_kv(g, carry):
        for x in (1, 2):
            for j in peers:
                kv_copy(x, j, g, me).start()
        return carry

    lax.fori_loop(0, heads, send_kv, 0)

    def sent_in(x, j):
        return pltpu.make_async_remote_copy(
            src_ref=ins[x].at[:, cols_of(j)],
            dst_ref=qb.at[rows_of(me), :],
            send_sem=in_send.at[x, j],
            recv_sem=qd_recv.at[0, 0, me],
            device_id=(c, j),
            device_id_type=MESH,
        )

    def look(t, carry):
        def items(it, found):
            block, group, filled = found
            g = lax.rem(it, GROUPS)
            m = match[g, t * here + it // GROUPS]
            hit = (m >= c * here) & (m < (c + 1) * here)
            return (
                jnp.where(hit, m - c * here, block),
                jnp.where(hit, g, group),
                jnp.where(hit, 1, filled),
            )

        block, group, filled = lax.fori_loop(0, here * GROUPS, items, (0, 0, 0))
        table[0, t] = block
        table[1, t] = group
        table[2, t] = filled
        return carry

    lax.fori_loop(c + 1, ctxs, look, 0)

    def serve(s, carry):
        def items(it, found):
            m = match[lax.rem(it, GROUPS), c * here + it // GROUPS]
            hit = (m >= s * here) & (m < (s + 1) * here)
            return jnp.where(hit, it, found)

        table[3, s] = lax.fori_loop(0, here * GROUPS, items, 0)
        return carry

    lax.fori_loop(0, c, serve, 0)

    for x in (1, 2):
        for j in peers:
            sent_in(x, j).wait_send()

    def qd_copy(x, j, g, row):
        y = 0 if x == 0 else 1
        return pltpu.make_async_remote_copy(
            src_ref=ins[x].at[:, wide_head(j, g)],
            dst_ref=bufs[x].at[rows_of(row), head_of(g)],
            send_sem=in_send.at[x, j],
            recv_sem=qd_recv.at[y, g, row],
            device_id=(c, j),
            device_id_type=MESH,
        )

    def send_qd(g, carry):
        for x in (0, 3):
            for j in peers:
                qd_copy(x, j, g, me).start()
        return carry

    lax.fori_loop(0, heads, send_qd, 0)

    def take_kv(g, carry):
        for x in (1, 2):
            for j in peers:
                kv_copy(x, j, g, j).wait_recv()
        return carry

    lax.fori_loop(0, heads, take_kv, 0)
    for x in (1, 2):
        pltpu.make_async_copy(
            ins[x].at[:, cols_of(me)], qb.at[rows_of(me), :], in_local.at[x]
        ).wait()

    def slot_copy(t, s):
        return pltpu.make_async_remote_copy(
            src_ref=pack.at[t],
            dst_ref=slots.at[s],
            send_sem=slot_send.at[t],
            recv_sem=slot_recv.at[s],
            device_id=(t, me),
            device_id_type=MESH,
        )

    def send_slot(t, carry):
        item = table[0, t] * heads + table[1, t]
        pack[t, 0] = kb[item]
        pack[t, 1] = vb[item]
        slot_copy(t, c).start()
        return carry

    lax.fori_loop(c + 1, ctxs, send_slot, 0)

    own_in(0).wait()
    own_in(3).wait()

    def take_slot(s, carry):
        slot_copy(s, s).wait_recv()
        return carry

    lax.fori_loop(0, c, take_slot, 0)

    scale = HEAD_DIM**-0.5
    key_at = lax.broadcasted_iota(jnp.int32, (BLOCK, BLOCK), 0)
    query_at = lax.broadcasted_iota(jnp.int32, (BLOCK, BLOCK), 1)

    def out_copy(o, j, g, col):
        return pltpu.make_async_remote_copy(
            src_ref=stages[o].at[rows_of(j), head_of(g)],
            dst_ref=outs[o].at[:, wide_head(col, g)],
            send_sem=out_send.at[o, j],
            recv_sem=out_recv.at[o, col],
            device_id=(c, j),
            device_id_type=MESH,
        )

    def own_out(o, g):
        return pltpu.make_async_copy(
            stages[o].at[rows_of(me), head_of(g)], outs[o].at[:, wide_head(me, g)], out_local.at[o]
        )

    def send_out(o, g):
        for j in peers:
            out_copy(o, j, g, me).start()
        own_out(o, g).start()

    def work(g, carry):
        for x in (0, 3):
            for j in peers:
                qd_copy(x, j, g, j).wait_recv()
        cols = head_of(g)
        totals = []
        for b in range(here):
            rows = pl.ds(b * BLOCK, BLOCK)
            q, do = qb[rows, cols], db[rows, cols]
            k, v = kb[b * heads + g], vb[b * heads + g]
            m = match[g, c * here + b]
            valid = m < c * here + b
            source = lax.div(m, here)
            fk, fv = slots[source, 0], slots[source, 1]
            for near in range(b + 1):
                hit = m == c * here + near
                fk = jnp.where(hit, kb[near * heads + g], fk)
                fv = jnp.where(hit, vb[near * heads + g], fv)
            s_own = jnp.where(key_at <= query_at, dot(k, q, (1, 1)) * (scale * LOG2E), -jnp.inf)
            s_far = dot(fk, q, (1, 1)) * (scale * LOG2E) + jnp.where(valid, 0.0, -jnp.inf)
            top = jnp.maximum(
                jnp.max(s_own, axis=0, keepdims=True), jnp.max(s_far, axis=0, keepdims=True)
            )
            e_own = jnp.exp2(s_own - top)
            e_far = jnp.exp2(s_far - top)
            inverse = 1.0 / (
                jnp.sum(e_own, axis=0, keepdims=True) + jnp.sum(e_far, axis=0, keepdims=True)
            )
            p_own = e_own * inverse
            p_far = e_far * inverse
            pb_own = p_own.astype(jnp.bfloat16)
            pb_far = p_far.astype(jnp.bfloat16)
            att = (dot(v, pb_own, (0, 0)) + dot(fv, pb_far, (0, 0))).astype(jnp.bfloat16)
            att = att.astype(jnp.float32)
            delta = jnp.sum(do.astype(jnp.float32).T * att, axis=0, keepdims=True)
            attb[rows, cols] = att.T.astype(jnp.bfloat16)
            ds_own = (p_own * (dot(v, do, (1, 1)) - delta) * scale).astype(jnp.bfloat16)
            ds_far = (p_far * (dot(fv, do, (1, 1)) - delta) * scale).astype(jnp.bfloat16)
            gq = dot(k, ds_own, (0, 0)) + dot(fk, ds_far, (0, 0))
            gqb[rows, cols] = gq.T.astype(jnp.bfloat16)
            gk_far = dot(ds_far, q, (1, 0))
            gv_far = dot(pb_far, do, (1, 0))
            gfar[b * GROUPS + g, 0] = gk_far.astype(jnp.bfloat16)
            gfar[b * GROUPS + g, 1] = gv_far.astype(jnp.bfloat16)
            gk32[rows, cols] = dot(ds_own, q, (1, 0))
            gv32[rows, cols] = dot(pb_own, do, (1, 0))
            for target in range(b):
                hit = m == c * here + target
                to = pl.ds(target * BLOCK, BLOCK)
                gk32[to, cols] += jnp.where(hit, gk_far, 0.0)
                gv32[to, cols] += jnp.where(hit, gv_far, 0.0)
        send_out(0, g)
        send_out(1, g)
        return carry

    lax.fori_loop(0, heads, work, 0)

    def ret_copy(s, t):
        return pltpu.make_async_remote_copy(
            src_ref=back.at[s],
            dst_ref=came.at[t],
            send_sem=ret_send.at[s],
            recv_sem=ret_recv.at[t],
            device_id=(s, me),
            device_id_type=MESH,
        )

    def send_back(s, carry):
        item = table[3, s]
        back[s, 0] = gfar[item, 0]
        back[s, 1] = gfar[item, 1]
        ret_copy(s, c).start()
        return carry

    lax.fori_loop(0, c, send_back, 0)

    def take_back(t, carry):
        ret_copy(t, t).wait_recv()
        return carry

    lax.fori_loop(c + 1, ctxs, take_back, 0)

    def finish(g, carry):
        cols = head_of(g)
        for b in range(here):
            rows = pl.ds(b * BLOCK, BLOCK)
            for x, total, stage in ((0, gk32, gkb), (1, gv32, gvb)):

                def add(t, held):
                    hit = (table[0, t] == b) & (table[1, t] == g) & (table[2, t] == 1)
                    return held + jnp.where(hit, came[t, x].astype(jnp.float32), 0.0)

                stage[rows, cols] = lax.fori_loop(c + 1, ctxs, add, total[rows, cols]).astype(
                    jnp.bfloat16
                )
        send_out(2, g)
        send_out(3, g)
        return carry

    lax.fori_loop(0, heads, finish, 0)

    for x in (0, 3):
        for j in peers:
            sent_in(x, j).wait_send()

    def slots_sent(t, carry):
        slot_copy(t, c).wait_send()
        return carry

    lax.fori_loop(c + 1, ctxs, slots_sent, 0)

    def backs_sent(s, carry):
        ret_copy(s, c).wait_send()
        return carry

    lax.fori_loop(0, c, backs_sent, 0)
    for o in range(4):
        pltpu.make_async_copy(
            stages[o].at[rows_of(me), :], outs[o].at[:, cols_of(me)], out_local.at[o]
        ).wait()
        for j in peers:
            whole = pltpu.make_async_remote_copy(
                src_ref=stages[o].at[rows_of(j), :],
                dst_ref=outs[o].at[:, cols_of(j)],
                send_sem=out_send.at[o, j],
                recv_sem=out_recv.at[o, j],
                device_id=(c, j),
                device_id_type=MESH,
            )
            whole.wait_send()
            whole.wait_recv()


def solution(mesh):
    n = mesh.shape["tp"]
    ctxs = mesh.shape["ctx"]

    def shards(queries, keys, values, dout, match):
        part, width_all = queries.shape
        tokens, width = part * n, width_all // n
        here = tokens // BLOCK
        heads = width // HEAD_DIM
        assert heads == GROUPS
        buf = pltpu.VMEM((tokens, width), jnp.bfloat16)
        tiles = pltpu.VMEM((here * heads, BLOCK, HEAD_DIM), jnp.bfloat16)
        wide = pltpu.VMEM((tokens, width), jnp.float32)
        pairs = pltpu.VMEM((ctxs, 2, BLOCK, HEAD_DIM), jnp.bfloat16)
        dma = pltpu.SemaphoreType.DMA
        anywhere = pl.BlockSpec(memory_space=pl.ANY)
        items = here * heads
        return pl.pallas_call(
            functools.partial(kernel, n, ctxs),
            out_shape=[jax.ShapeDtypeStruct((part, width_all), jnp.bfloat16)] * 4,
            in_specs=[pl.BlockSpec(memory_space=pltpu.SMEM)] + [anywhere] * 4,
            out_specs=[anywhere] * 4,
            scratch_shapes=[buf, tiles, tiles, buf]
            + [buf] * 4
            + [wide] * 2
            + [pltpu.VMEM((items, 2, BLOCK, HEAD_DIM), jnp.bfloat16)]
            + [pairs] * 4
            + [
                pltpu.SMEM((4, ctxs), jnp.int32),
                dma((4, n)),
                dma((2, heads, n)),
                dma((2, heads, n)),
                dma((4,)),
                dma((ctxs,)),
                dma((ctxs,)),
                dma((ctxs,)),
                dma((ctxs,)),
                dma((4, n)),
                dma((4, n)),
                dma((4,)),
            ],
            compiler_params=pltpu.CompilerParams(
                collective_id=0, has_side_effects=True, vmem_limit_bytes=56 * 1024 * 1024
            ),
            cost_estimate=pl.CostEstimate(
                flops=12 * items * 2 * BLOCK * BLOCK * HEAD_DIM,
                bytes_accessed=16 * tokens * width,
                transcendentals=2 * items * BLOCK * BLOCK,
            ),
            name="matched_blocks",
        )(match, queries, keys, values, dout)

    split = P(("ctx", "tp"), None)
    return jax.shard_map(
        shards,
        mesh=mesh,
        in_specs=(split, split, split, split, P()),
        out_specs=(split,) * 4,
        check_vma=False,
    )
```

```python
import functools

import jax
import jax.numpy as jnp
from jax import lax
from jax.experimental import pallas as pl
from jax.experimental.pallas import tpu as pltpu
from jax.sharding import PartitionSpec as P

HEAD_DIM = 128
BLOCK = 256
GROUPS = 10
MESH = pl.DeviceIdType.MESH
LOG2E = 1.4426950408889634


def dot(a, b, dims):
    return lax.dot_general(a, b, ((dims[:1], dims[1:]), ((), ())), preferred_element_type=jnp.float32)


def kernel(
    n,
    ctxs,
    match,
    q_ref,
    k_ref,
    v_ref,
    d_ref,
    att_ref,
    gq_ref,
    gk_ref,
    gv_ref,
    qb,
    kb,
    vb,
    db,
    attb,
    gqb,
    gkb,
    gvb,
    gk32,
    gv32,
    gfar,
    pack,
    slots,
    back,
    came,
    table,
    in_send,
    kv_recv,
    qd_recv,
    in_local,
    slot_send,
    slot_recv,
    ret_send,
    ret_recv,
    out_send,
    out_recv,
    out_local,
):
    c = lax.axis_index("ctx")
    me = lax.axis_index("tp")
    part = q_ref.shape[0]
    width = qb.shape[1]
    here = qb.shape[0] // BLOCK
    heads = width // HEAD_DIM
    shares = BLOCK // part
    peers = [lax.rem(me + d, n) for d in range(1, n)]

    def rows_of(j):
        return pl.ds(pl.multiple_of(j * part, part), part)

    def cols_of(j):
        return pl.ds(pl.multiple_of(j * width, width), width)

    def head_of(g):
        return pl.ds(pl.multiple_of(g * HEAD_DIM, HEAD_DIM), HEAD_DIM)

    def wide_head(j, g):
        return pl.ds(pl.multiple_of(j * width + g * HEAD_DIM, HEAD_DIM), HEAD_DIM)

    ins = (q_ref, k_ref, v_ref, d_ref)
    bufs = (qb, kb, vb, db)
    outs = (att_ref, gq_ref, gk_ref, gv_ref)
    stages = (attb, gqb, gkb, gvb)

    barrier = pltpu.get_barrier_semaphore()
    for j in peers:
        pl.semaphore_signal(barrier, inc=1, device_id=(c, j), device_id_type=MESH)

    def greet(step, carry):
        pl.semaphore_signal(
            barrier, inc=1, device_id=(lax.rem(c + step, ctxs), me), device_id_type=MESH
        )
        return carry

    lax.fori_loop(1, ctxs, greet, 0)
    def own_in(x):
        return pltpu.make_async_copy(
            ins[x].at[:, cols_of(me)], bufs[x].at[rows_of(me), :], in_local.at[x]
        )

    for x in (0, 3):
        own_in(x).start()

    def kv_place(x, j, g):
        half = pl.multiple_of(lax.rem(j, shares) * part, part)
        return bufs[x].at[(j // shares) * heads + g, pl.ds(half, part), :]

    def own_kv(x, g):
        return pltpu.make_async_copy(
            ins[x].at[:, wide_head(me, g)], kv_place(x, me, g), in_local.at[x]
        )

    def start_own_kv(g, carry):
        for x in (1, 2):
            own_kv(x, g).start()
        return carry

    lax.fori_loop(0, heads, start_own_kv, 0)

    pl.semaphore_wait(barrier, n - 1 + ctxs - 1)

    def kv_copy(x, j, g, row):
        return pltpu.make_async_remote_copy(
            src_ref=ins[x].at[:, wide_head(j, g)],
            dst_ref=kv_place(x, row, g),
            send_sem=in_send.at[x, j],
            recv_sem=kv_recv.at[x - 1, g, row],
            device_id=(c, j),
            device_id_type=MESH,
        )

    def send_kv(g, carry):
        for x in (1, 2):
            for j in peers:
                kv_copy(x, j, g, me).start()
        return carry

    lax.fori_loop(0, heads, send_kv, 0)

    def sent_in(x, j):
        return pltpu.make_async_remote_copy(
            src_ref=ins[x].at[:, cols_of(j)],
            dst_ref=qb.at[rows_of(me), :],
            send_sem=in_send.at[x, j],
            recv_sem=qd_recv.at[0, 0, me],
            device_id=(c, j),
            device_id_type=MESH,
        )

    def qd_copy(x, j, g, row):
        y = 0 if x == 0 else 1
        return pltpu.make_async_remote_copy(
            src_ref=ins[x].at[:, wide_head(j, g)],
            dst_ref=bufs[x].at[rows_of(row), head_of(g)],
            send_sem=in_send.at[x, j],
            recv_sem=qd_recv.at[y, g, row],
            device_id=(c, j),
            device_id_type=MESH,
        )

    def send_qd(g, carry):
        for x in (0, 3):
            for j in peers:
                qd_copy(x, j, g, me).start()
        return carry

    for j in peers:
        sent_in(1, j).wait_send()
    lax.fori_loop(0, heads, send_qd, 0)

    def look(t, carry):
        def items(it, found):
            block, group, filled = found
            g = lax.rem(it, GROUPS)
            m = match[g, t * here + it // GROUPS]
            hit = (m >= c * here) & (m < (c + 1) * here)
            return (
                jnp.where(hit, m - c * here, block),
                jnp.where(hit, g, group),
                jnp.where(hit, 1, filled),
            )

        block, group, filled = lax.fori_loop(0, here * GROUPS, items, (0, 0, 0))
        table[0, t] = block
        table[1, t] = group
        table[2, t] = filled
        return carry

    lax.fori_loop(c + 1, ctxs, look, 0)

    def serve(s, carry):
        def items(it, found):
            m = match[lax.rem(it, GROUPS), c * here + it // GROUPS]
            hit = (m >= s * here) & (m < (s + 1) * here)
            return jnp.where(hit, it, found)

        table[3, s] = lax.fori_loop(0, here * GROUPS, items, 0)
        return carry

    lax.fori_loop(0, c, serve, 0)

    def take_kv(g, carry):
        for x in (1, 2):
            for j in peers:
                kv_copy(x, j, g, j).wait_recv()
        return carry

    lax.fori_loop(0, heads, take_kv, 0)
    for x in (1, 2):
        pltpu.make_async_copy(
            ins[x].at[:, cols_of(me)], qb.at[rows_of(me), :], in_local.at[x]
        ).wait()

    def slot_copy(t, s):
        return pltpu.make_async_remote_copy(
            src_ref=pack.at[t],
            dst_ref=slots.at[s],
            send_sem=slot_send.at[t],
            recv_sem=slot_recv.at[s],
            device_id=(t, me),
            device_id_type=MESH,
        )

    def send_slot(t, carry):
        item = table[0, t] * heads + table[1, t]
        pack[t, 0] = kb[item]
        pack[t, 1] = vb[item]
        slot_copy(t, c).start()
        return carry

    lax.fori_loop(c + 1, ctxs, send_slot, 0)

    own_in(0).wait()
    own_in(3).wait()

    def take_slot(s, carry):
        slot_copy(s, s).wait_recv()
        return carry

    lax.fori_loop(0, c, take_slot, 0)

    scale = HEAD_DIM**-0.5
    key_at = lax.broadcasted_iota(jnp.int32, (BLOCK, BLOCK), 0)
    query_at = lax.broadcasted_iota(jnp.int32, (BLOCK, BLOCK), 1)

    def out_copy(o, j, g, col):
        return pltpu.make_async_remote_copy(
            src_ref=stages[o].at[rows_of(j), head_of(g)],
            dst_ref=outs[o].at[:, wide_head(col, g)],
            send_sem=out_send.at[o, j],
            recv_sem=out_recv.at[o, col],
            device_id=(c, j),
            device_id_type=MESH,
        )

    def own_out(o, g):
        return pltpu.make_async_copy(
            stages[o].at[rows_of(me), head_of(g)], outs[o].at[:, wide_head(me, g)], out_local.at[o]
        )

    def send_out(o, g):
        for j in peers:
            out_copy(o, j, g, me).start()
        own_out(o, g).start()

    def work(g, carry):
        for x in (0, 3):
            for j in peers:
                qd_copy(x, j, g, j).wait_recv()
        cols = head_of(g)
        totals = []
        for b in range(here):
            rows = pl.ds(b * BLOCK, BLOCK)
            q, do = qb[rows, cols], db[rows, cols]
            k, v = kb[b * heads + g], vb[b * heads + g]
            m = match[g, c * here + b]
            valid = m < c * here + b
            source = lax.div(m, here)
            fk, fv = slots[source, 0], slots[source, 1]
            for near in range(b + 1):
                hit = m == c * here + near
                fk = jnp.where(hit, kb[near * heads + g], fk)
                fv = jnp.where(hit, vb[near * heads + g], fv)
            s_own = jnp.where(key_at <= query_at, dot(k, q, (1, 1)) * (scale * LOG2E), -jnp.inf)
            s_far = dot(fk, q, (1, 1)) * (scale * LOG2E) + jnp.where(valid, 0.0, -jnp.inf)
            top = jnp.maximum(
                jnp.max(s_own, axis=0, keepdims=True), jnp.max(s_far, axis=0, keepdims=True)
            )
            e_own = jnp.exp2(s_own - top)
            e_far = jnp.exp2(s_far - top)
            inverse = 1.0 / (
                jnp.sum(e_own, axis=0, keepdims=True) + jnp.sum(e_far, axis=0, keepdims=True)
            )
            p_own = e_own * inverse
            p_far = e_far * inverse
            pb_own = p_own.astype(jnp.bfloat16)
            pb_far = p_far.astype(jnp.bfloat16)
            att = (dot(v, pb_own, (0, 0)) + dot(fv, pb_far, (0, 0))).astype(jnp.bfloat16)
            att = att.astype(jnp.float32)
            delta = jnp.sum(do.astype(jnp.float32).T * att, axis=0, keepdims=True)
            attb[rows, cols] = att.T.astype(jnp.bfloat16)
            ds_own = (p_own * (dot(v, do, (1, 1)) - delta) * scale).astype(jnp.bfloat16)
            ds_far = (p_far * (dot(fv, do, (1, 1)) - delta) * scale).astype(jnp.bfloat16)
            gq = dot(k, ds_own, (0, 0)) + dot(fk, ds_far, (0, 0))
            gqb[rows, cols] = gq.T.astype(jnp.bfloat16)
            gk_far = dot(ds_far, q, (1, 0))
            gv_far = dot(pb_far, do, (1, 0))
            gfar[b * GROUPS + g, 0] = gk_far.astype(jnp.bfloat16)
            gfar[b * GROUPS + g, 1] = gv_far.astype(jnp.bfloat16)
            gk32[rows, cols] = dot(ds_own, q, (1, 0))
            gv32[rows, cols] = dot(pb_own, do, (1, 0))
            for target in range(b):
                hit = m == c * here + target
                to = pl.ds(target * BLOCK, BLOCK)
                gk32[to, cols] += jnp.where(hit, gk_far, 0.0)
                gv32[to, cols] += jnp.where(hit, gv_far, 0.0)
        send_out(0, g)
        send_out(1, g)
        return carry

    lax.fori_loop(0, heads, work, 0)

    def ret_copy(s, t):
        return pltpu.make_async_remote_copy(
            src_ref=back.at[s],
            dst_ref=came.at[t],
            send_sem=ret_send.at[s],
            recv_sem=ret_recv.at[t],
            device_id=(s, me),
            device_id_type=MESH,
        )

    def send_back(s, carry):
        item = table[3, s]
        back[s, 0] = gfar[item, 0]
        back[s, 1] = gfar[item, 1]
        ret_copy(s, c).start()
        return carry

    lax.fori_loop(0, c, send_back, 0)

    def take_back(t, carry):
        ret_copy(t, t).wait_recv()
        return carry

    lax.fori_loop(c + 1, ctxs, take_back, 0)

    def finish(g, carry):
        cols = head_of(g)
        for b in range(here):
            rows = pl.ds(b * BLOCK, BLOCK)
            for x, total, stage in ((0, gk32, gkb), (1, gv32, gvb)):

                def add(t, held):
                    hit = (table[0, t] == b) & (table[1, t] == g) & (table[2, t] == 1)
                    return held + jnp.where(hit, came[t, x].astype(jnp.float32), 0.0)

                stage[rows, cols] = lax.fori_loop(c + 1, ctxs, add, total[rows, cols]).astype(
                    jnp.bfloat16
                )
        send_out(2, g)
        send_out(3, g)
        return carry

    lax.fori_loop(0, heads, finish, 0)

    for x in (0, 2, 3):
        for j in peers:
            sent_in(x, j).wait_send()

    def slots_sent(t, carry):
        slot_copy(t, c).wait_send()
        return carry

    lax.fori_loop(c + 1, ctxs, slots_sent, 0)

    def backs_sent(s, carry):
        ret_copy(s, c).wait_send()
        return carry

    lax.fori_loop(0, c, backs_sent, 0)
    for o in range(4):
        pltpu.make_async_copy(
            stages[o].at[rows_of(me), :], outs[o].at[:, cols_of(me)], out_local.at[o]
        ).wait()
        for j in peers:
            whole = pltpu.make_async_remote_copy(
                src_ref=stages[o].at[rows_of(j), :],
                dst_ref=outs[o].at[:, cols_of(j)],
                send_sem=out_send.at[o, j],
                recv_sem=out_recv.at[o, j],
                device_id=(c, j),
                device_id_type=MESH,
            )
            whole.wait_send()
            whole.wait_recv()


def solution(mesh):
    n = mesh.shape["tp"]
    ctxs = mesh.shape["ctx"]

    def shards(queries, keys, values, dout, match):
        part, width_all = queries.shape
        tokens, width = part * n, width_all // n
        here = tokens // BLOCK
        heads = width // HEAD_DIM
        assert heads == GROUPS
        buf = pltpu.VMEM((tokens, width), jnp.bfloat16)
        tiles = pltpu.VMEM((here * heads, BLOCK, HEAD_DIM), jnp.bfloat16)
        wide = pltpu.VMEM((tokens, width), jnp.float32)
        pairs = pltpu.VMEM((ctxs, 2, BLOCK, HEAD_DIM), jnp.bfloat16)
        dma = pltpu.SemaphoreType.DMA
        anywhere = pl.BlockSpec(memory_space=pl.ANY)
        items = here * heads
        held = tokens * width * 24 + (items + 4 * ctxs) * 2 * BLOCK * HEAD_DIM * 2
        return pl.pallas_call(
            functools.partial(kernel, n, ctxs),
            out_shape=[jax.ShapeDtypeStruct((part, width_all), jnp.bfloat16)] * 4,
            in_specs=[pl.BlockSpec(memory_space=pltpu.SMEM)] + [anywhere] * 4,
            out_specs=[anywhere] * 4,
            scratch_shapes=[buf, tiles, tiles, buf]
            + [buf] * 4
            + [wide] * 2
            + [pltpu.VMEM((items, 2, BLOCK, HEAD_DIM), jnp.bfloat16)]
            + [pairs] * 4
            + [
                pltpu.SMEM((4, ctxs), jnp.int32),
                dma((4, n)),
                dma((2, heads, n)),
                dma((2, heads, n)),
                dma((4,)),
                dma((ctxs,)),
                dma((ctxs,)),
                dma((ctxs,)),
                dma((ctxs,)),
                dma((4, n)),
                dma((4, n)),
                dma((4,)),
            ],
            compiler_params=pltpu.CompilerParams(
                collective_id=0, has_side_effects=True, vmem_limit_bytes=held + 9 * 1024 * 1024
            ),
            cost_estimate=pl.CostEstimate(
                flops=12 * items * 2 * BLOCK * BLOCK * HEAD_DIM,
                bytes_accessed=16 * tokens * width,
                transcendentals=2 * items * BLOCK * BLOCK,
            ),
            name="matched_blocks",
        )(
            match,
            *(pltpu.with_memory_space_constraint(x, pltpu.HBM) for x in (queries, keys, values, dout)),
        )

    split = P(("ctx", "tp"), None)
    return jax.shard_map(
        shards,
        mesh=mesh,
        in_specs=(split, split, split, split, P()),
        out_specs=(split,) * 4,
        check_vma=False,
    )
```
